32 devices in a mesh: batch: 2 (over y), aux: 4 (over z), ao: 4 (over x, core).
Axes of the slice: x: 2, y: 2, z: 4, core: 2. Of those that a mesh axis runs over, the one named last changes fastest.
Arguments:
- pair_ints: bfloat16 [8, 96, 20480], P(('batch', 'ao'), 'aux'), parts along dimension 0, may hold values from -6 to 6
- batch_energy: float32 [8], P(('batch', 'ao')), parts along dimension 0, may hold values from 0.3 to 3
- occ_energy: float32 [96], P('aux'), may hold values from 0.3 to 3
- occ_coef: bfloat16 [6144, 96], P('ao', 'aux'), may hold values from -0.625 to 0.625
- batch_coef: bfloat16 [6144, 8], P('ao', 'batch'), parts along dimension 1, may hold values from -3 to 3
- deriv: bfloat16 [3, 6144, 20480], P(None, 'ao', 'aux'), may hold values from -0.0390625 to 0.0390625
- owner: int32 [6144], P('ao'), may hold values from 0 to 47, never falling along the last dimension, each value on 1 to 384 neighbouring positions
Outputs:
- amp_ao: bfloat16 [12288, 20480], P(('batch', 'ao'), 'aux'), parts along dimension 0
- gradient: float32 [3, 96], P(None, ('batch', 'aux', 'ao')), parts along dimension 1
The draws below stay inside these ranges and needn't reach their ends.
There are 2 independent parts, one for each index of `batch`. The reference program is written for one: setup_inputs(seed, part) draws one part's arguments, and reference() takes and returns one part's arrays. A program takes and returns all parts, laid end to end along the dimension named above; an argument that names none is the same for every part. Nothing has to cross between parts.
Inputs may be any that keep to these rules, and one draw needn't show every extreme that they name: `owner`: never falls along the AO functions; every atom owns 1 to 384 functions, some atom exactly 384.
All inputs are finite; a program needn't handle non-finite values.
Results may differ from the reference program's by a relative error of at most 0.0051.
Values may be sent and summed in bfloat16 or wider, within the bound.
A program may use at most 320 MiB of HBM per device.

```python
import math
import jax
import jax.numpy as jnp
import numpy as np
from jax import lax

NI = 4
NOCC = 96
NAUX = 20480
NAO = 6144
NATOM = 48
ATOM_MOST = 384


def block_scale(rng, dims, shards, smallest, top_value):
    factor_of = 1.0
    for dim, parts in shards:
        steps = jax.random.uniform(jax.random.fold_in(jax.random.fold_in(rng, 6), dim), (parts,), jnp.float32, smallest / len(shards), top_value / len(shards))
        factor_of = factor_of * jnp.repeat(jnp.exp(steps), dims[dim] // parts).reshape((-1,) + (1,) * (len(dims) - 1 - dim))
    return factor_of


def length_profile(count, total, reach, lean):
    loads = [(1 << 20) // math.isqrt(standing ** lean) + 1 for standing in range(2, count + 1)]
    surplus, counts = total - reach - (count - 1), [1] * (count - 1)
    while surplus > 0:
        candidates = [i for i in range(count - 1) if counts[i] < reach]
        mass, budget = sum([loads[i] for i in candidates]), surplus
        for i in candidates:
            extra = min(reach - counts[i], max(1, budget * loads[i] // mass), surplus)
            counts[i] = counts[i] + extra
            surplus = surplus - extra
    return np.array([reach] + counts)


def uneven_parts(key, amount, total, most, skew):
    if amount == 2:
        one = jax.random.randint(key, (), max(1, total - most), min(most, total - 1) + 1)
        return jnp.stack([one, total - one])
    tallies = jnp.asarray(length_profile(amount, total, most, skew), jnp.int32)
    twos = (amount - 1) // 2
    source_of, receiver = tallies[1:1 + 2 * twos:2], tallies[2:2 + 2 * twos:2]
    margin = jnp.minimum(source_of - 1, most - receiver)
    shifted = jax.random.randint(jax.random.fold_in(key, 1), (twos,), 0, 1 << 20) % (margin + 1)
    tallies = tallies.at[1:1 + 2 * twos:2].set(source_of - shifted).at[2:2 + 2 * twos:2].set(receiver + shifted)
    return tallies[jax.random.permutation(jax.random.fold_in(key, 2), amount)]


def normal_values(stream_key, extent, width, most, cuts=(), held_as=jnp.bfloat16):
    result = jax.random.normal(stream_key, extent, jnp.float32) * width
    if len(cuts) > 0:
        result = block_scale(stream_key, extent, cuts, -0.22, 0.18) * result
    return jnp.clip(result, min=-most, max=most).astype(held_as)


def setup_inputs(seed: int = 0, part: int = 0) -> dict:
    key_of = jax.random.split(jax.random.key(seed), 8)
    part_splits = jax.random.split(jax.random.fold_in(key_of[7], part), 8)
    pair_ints = normal_values(part_splits[0], (NI, NOCC, NAUX), 1.0, 6.0, ((0, 4), (1, 4)))
    batch_energy = jnp.clip(jnp.exp(math.log(3.0) - 2.3025851 * jax.random.uniform(part_splits[1], (NI,), jnp.float32) ** block_scale(part_splits[1], (NI,), ((0, 4),), -0.2, 0.2)), 0.3, 3.0)
    occ_energy = jnp.clip(jnp.exp(math.log(3.0) - 2.3025851 * jax.random.uniform(key_of[2], (NOCC,), jnp.float32) ** block_scale(key_of[2], (NOCC,), ((0, 4),), -0.2, 0.2)), 0.3, 3.0)
    occ_coef = normal_values(key_of[3], (NAO, NOCC), NOCC ** -0.5, 0.625, ((0, 4), (1, 4)))
    batch_coef = normal_values(part_splits[4], (NAO, NI), NI ** -0.5, 3.0, ((0, 4),))
    deriv = normal_values(key_of[5], (3, NAO, NAUX), NAUX ** -0.5, 0.0390625, ((1, 4), (2, 4)))
    owner = jnp.searchsorted(jnp.cumsum(uneven_parts(key_of[6], NATOM, NAO, ATOM_MOST, 2)), jnp.arange(NAO), side="right").astype(jnp.int32)
    return {"pair_ints": pair_ints, "batch_energy": batch_energy, "occ_energy": occ_energy, "occ_coef": occ_coef, "batch_coef": batch_coef, "deriv": deriv, "owner": owner}


def reference(pair_ints, batch_energy, occ_energy, occ_coef, batch_coef, deriv, owner):
    scale = 2.0 / (batch_energy[:, None] + occ_energy[None, :])
    formed = (pair_ints.astype(jnp.float32) * scale[:, :, None]).astype(jnp.bfloat16)
    summed = jnp.zeros((NAO, NAUX), jnp.float32)
    for orbit in range(NI):
        half_ao = jnp.dot(occ_coef, formed[orbit], preferred_element_type=jnp.float32)
        summed = summed + batch_coef[:, orbit].astype(jnp.float32)[:, None] * half_ao
    amp_ao = summed.astype(jnp.bfloat16)
    amp_wide = amp_ao.astype(jnp.float32)
    rows = []
    for axis_dir in range(3):
        rows.append(jnp.sum(deriv[axis_dir].astype(jnp.float32) * amp_wide, axis=1))
    per_func = jnp.stack(rows, 0)
    onehot = (owner[:, None] == jnp.arange(NATOM, dtype=jnp.int32)[None, :]).astype(jnp.float32)
    gradient = jnp.dot(per_func, onehot, precision=lax.Precision.HIGHEST)
    return amp_ao, gradient
```

```python
import functools

import jax
import jax.numpy as jnp
from jax import lax
from jax.experimental import pallas as pl
from jax.experimental.pallas import tpu as pltpu
from jax.sharding import PartitionSpec as P

ATOM_DEV = 3
MESH = pl.DeviceIdType.MESH
F32 = jnp.float32
BF16 = jnp.bfloat16
CHUNK = 512
ROWS = 256
SLOTS = 3
LEAVE = 8


def eye(rows, columns, dtype):
    row = lax.broadcasted_iota(jnp.int32, (rows, columns), 0)
    column = lax.broadcasted_iota(jnp.int32, (rows, columns), 1)
    return (row == column).astype(F32).astype(dtype)


def across(left, right, **kw):
    return lax.dot_general(
        left, right, (((1,), (1,)), ((), ())), preferred_element_type=F32, **kw
    )


def fused_kernel(
    aux, atoms, pair, batch_energy, occ_energy, occ_coef, batch_coef, deriv, owner,
    amp, grad,
    outgoing, arrived, coef, coef_t, weights, packed, slabs, total,
    z_send, z_recv, w_send, w_recv, x_send, x_recv, c_send, c_recv, f_send, f_recv, d_sem,
):
    occ = pair.shape[1]
    width = pair.shape[2] // aux
    chunks = width // CHUNK
    half = CHUNK // 2
    functions = occ_coef.shape[0]
    me_z, me = lax.axis_index("aux"), lax.axis_index("ao")
    far = lax.rem(me + 2, 4)
    near = me + 1 - 2 * lax.rem(me, 2)
    near_far = lax.rem(near + 2, 4)

    def fetch(step):
        return pltpu.make_async_copy(
            deriv.at[:, :, pl.ds(step * CHUNK, CHUNK)], slabs.at[step % SLOTS], d_sem.at[step % SLOTS]
        )

    for step in range(min(SLOTS, chunks)):
        fetch(step).start()

    barrier = pltpu.get_barrier_semaphore()
    for hop in range(1, aux):
        pl.semaphore_signal(
            barrier, inc=1, device_id={"aux": lax.rem(me_z + hop, aux)}, device_id_type=MESH
        )
    for other in (far, near):
        pl.semaphore_signal(barrier, inc=1, device_id={"ao": other}, device_id_type=MESH)

    turned = across(eye(occ, occ, BF16), occ_coef[...])
    coef[me_z] = jnp.concatenate(
        [turned[:, : functions // 2], turned[:, functions // 2 :]], axis=0
    ).astype(BF16)

    scale_row = 2.0 / (batch_energy[0] + occ_energy[...])
    scale = jnp.sum(eye(occ, occ, F32) * scale_row, axis=1, keepdims=True)

    def form(z, step):
        start = pl.multiple_of(z * width + step * CHUNK, CHUNK)
        block = pair[0, :, pl.ds(start, CHUNK)].astype(F32) * scale
        return jnp.concatenate([block[:, :half], block[:, half:]], axis=0).astype(BF16)

    def z_copy(step, hop, source=None):
        z = me_z if source is None else source
        return pltpu.make_async_remote_copy(
            src_ref=outgoing.at[hop - 1, step],
            dst_ref=arrived.at[step, me, z],
            send_sem=z_send.at[step, hop - 1],
            recv_sem=z_recv.at[step, hop - 1],
            device_id={"aux": lax.rem(me_z + hop, aux)},
            device_id_type=MESH,
        )

    def w_copy(hop, source=None):
        z = me_z if source is None else source
        return pltpu.make_async_remote_copy(
            src_ref=coef.at[me_z],
            dst_ref=coef.at[z],
            send_sem=w_send.at[hop - 1],
            recv_sem=w_recv.at[hop - 1],
            device_id={"aux": lax.rem(me_z + hop, aux)},
            device_id_type=MESH,
        )

    def slot_copy(step, slot, sends, recvs, target, source=None):
        return pltpu.make_async_remote_copy(
            src_ref=arrived.at[step, slot],
            dst_ref=arrived.at[step, slot if source is None else source],
            send_sem=sends.at[step],
            recv_sem=recvs.at[step],
            device_id={"ao": target},
            device_id_type=MESH,
        )

    def x_copy(step, source=None):
        return slot_copy(step, me, x_send, x_recv, far, source)

    def c_copy(step, source=None):
        return slot_copy(step, me, c_send, c_recv, near, source)

    def f_copy(step, source=None):
        return slot_copy(step, far, f_send, f_recv, near, source)

    def send_chunk(step):
        for hop in range(1, aux):
            outgoing[hop - 1, step] = form(lax.rem(me_z + hop, aux), step)
            z_copy(step, hop).start()
        arrived[step, me, me_z] = form(me_z, step)

    def behind(hop):
        return lax.rem(me_z + aux - hop, aux)

    pl.semaphore_wait(barrier, aux + 1)
    send_chunk(0)
    for hop in range(1, aux):
        w_copy(hop).start()
    for step in range(1, chunks):
        send_chunk(step)

    total[...] = jnp.zeros_like(total)
    columns = across(eye(8, batch_coef.shape[1], BF16), batch_coef[...])

    def build_weights():
        for hop in range(1, aux):
            w_copy(hop, behind(hop)).wait_recv()
        for part in range(2):
            lanes = slice(part * (functions // 2), (part + 1) * (functions // 2))
            for z in range(aux):
                block = coef[z].astype(F32)[part * occ : (part + 1) * occ]
                for orbit in range(4):
                    first = (orbit * aux + z) * occ
                    coef_t[first : first + occ, :] = block * columns[orbit : orbit + 1, lanes]
            weights[lanes, :] = coef_t[...].T.astype(BF16)

    def compute(step):
        for pair_of in range(2 * aux):
            blocks = [
                arrived[step, source // aux, source % aux].astype(F32)
                for source in (2 * pair_of, 2 * pair_of + 1)
            ]
            for part in range(2):
                packed[2 * occ * pair_of : 2 * occ * (pair_of + 1), part * half : (part + 1) * half] = (
                    jnp.concatenate(
                        [block[part * occ : (part + 1) * occ] for block in blocks], axis=0
                    ).astype(BF16)
                )
        fetch(step).wait()
        slab = slabs.at[step % SLOTS]

        @pl.loop(0, functions // ROWS)
        def _(index):
            rows = pl.ds(pl.multiple_of(index * ROWS, ROWS), ROWS)
            rounded = jnp.dot(
                weights[rows, :], packed[...], preferred_element_type=F32
            ).astype(BF16)
            amp[rows, step * CHUNK : (step + 1) * CHUNK] = rounded
            wide = rounded.astype(F32)
            for axis_dir in range(3):
                product = slab[axis_dir, rows, :].astype(F32) * wide
                lanes = product[:, :128]
                for first in range(128, CHUNK, 128):
                    lanes = lanes + product[:, first : first + 128]
                total[axis_dir, rows, :] += lanes

        if step + SLOTS < chunks:
            fetch(step + SLOTS).start()

    for turn in range(chunks + 2):
        if turn < chunks:
            for hop in range(1, aux):
                z_copy(turn, hop, behind(hop)).wait_recv()
            x_copy(turn).start()
            c_copy(turn).start()
        if turn == 0:
            build_weights()
        if 1 <= turn <= chunks:
            x_copy(turn - 1, far).wait_recv()
            f_copy(turn - 1).start()
        if turn >= 2:
            c_copy(turn - 2, near).wait_recv()
            f_copy(turn - 2, near_far).wait_recv()
            compute(turn - 2)

    atom = lax.broadcasted_iota(jnp.int32, (atoms, functions), 0)
    onehot = (owner[...] == atom).astype(F32)
    sums = jnp.concatenate(
        [
            jnp.dot(onehot, total[axis_dir], precision=lax.Precision.HIGHEST, preferred_element_type=F32)
            for axis_dir in range(3)
        ],
        axis=0,
    )
    grad[...] = across(jnp.ones((8, 128), F32), sums, precision=lax.Precision.HIGHEST)

    for hop in range(1, aux):
        w_copy(hop).wait_send()
    for step in range(chunks):
        for hop in range(1, aux):
            z_copy(step, hop).wait_send()
        x_copy(step).wait_send()
        c_copy(step).wait_send()
        f_copy(step).wait_send()


def leave_kernel(held, out, sems):
    rows = held.shape[0] // LEAVE
    copies = [
        pltpu.make_async_copy(
            held.at[pl.ds(part * rows, rows)], out.at[pl.ds(part * rows, rows)], sems.at[part]
        )
        for part in range(LEAVE)
    ]
    for copy in copies:
        copy.start()
    for copy in copies:
        copy.wait()


def fused(aux, pair_ints, batch_energy, occ_energy, occ_coef, batch_coef, deriv, owner):
    occ = pair_ints.shape[1]
    functions, width = deriv.shape[1], deriv.shape[2]
    chunks = width // CHUNK
    atoms = ATOM_DEV * aux * 4
    depth = 4 * aux * occ
    vmem = pl.BlockSpec(memory_space=pltpu.VMEM)
    dma = pltpu.SemaphoreType.DMA
    amp, grad = pl.pallas_call(
        functools.partial(fused_kernel, aux, atoms),
        out_shape=(
            pltpu.VMEM((functions, width), BF16),
            jax.ShapeDtypeStruct((8, 3 * atoms), F32),
        ),
        in_specs=[
            vmem,
            pl.BlockSpec(memory_space=pltpu.SMEM),
            vmem,
            vmem,
            vmem,
            pl.BlockSpec(memory_space=pl.ANY),
            vmem,
        ],
        out_specs=(vmem, vmem),
        scratch_shapes=[
            pltpu.VMEM((aux - 1, chunks, 2 * occ, CHUNK // 2), BF16),
            pltpu.VMEM((chunks, 4, aux, 2 * occ, CHUNK // 2), BF16),
            pltpu.VMEM((aux, 2 * occ, functions // 2), BF16),
            pltpu.VMEM((depth, functions // 2), F32),
            pltpu.VMEM((functions, depth), BF16),
            pltpu.VMEM((depth, CHUNK), BF16),
            pltpu.VMEM((SLOTS, 3, functions, CHUNK), BF16),
            pltpu.VMEM((3, functions, 128), F32),
            dma((chunks, aux - 1)),
            dma((chunks, aux - 1)),
            dma((aux - 1,)),
            dma((aux - 1,)),
            dma((chunks,)),
            dma((chunks,)),
            dma((chunks,)),
            dma((chunks,)),
            dma((chunks,)),
            dma((chunks,)),
            dma((SLOTS,)),
        ],
        compiler_params=pltpu.CompilerParams(
            collective_id=0, has_side_effects=True, vmem_limit_bytes=42 << 20
        ),
    )(
        pair_ints,
        batch_energy,
        occ_energy.reshape(1, -1),
        occ_coef,
        batch_coef,
        deriv,
        owner.reshape(1, -1),
    )
    amp = pl.pallas_call(
        leave_kernel,
        out_shape=jax.ShapeDtypeStruct((functions, width), BF16),
        in_specs=[vmem],
        out_specs=pl.BlockSpec(memory_space=pl.ANY),
        scratch_shapes=[dma((LEAVE,))],
        compiler_params=pltpu.CompilerParams(vmem_limit_bytes=1 << 20),
    )(amp)
    totals = lax.psum(grad[:1], ("aux", "ao")).reshape(3, atoms)
    own = lax.axis_index(("aux", "ao")) * ATOM_DEV
    return amp, lax.dynamic_slice_in_dim(totals, own, ATOM_DEV, 1)


def staged(pair_ints, batch_energy, occ_energy, occ_coef, batch_coef, deriv, owner):
    scale = 2.0 / (batch_energy[:, None] + occ_energy[None, :])
    formed = (pair_ints.astype(F32) * scale[:, :, None]).astype(BF16)
    arrived = lax.all_to_all(formed, "aux", split_axis=2, concat_axis=1, tiled=True)
    coef_all = lax.all_gather(occ_coef, "aux", axis=1, tiled=True)
    column = batch_coef.astype(F32)
    gathered = lax.all_gather(arrived, "ao", axis=0, tiled=True)
    running = jnp.zeros((coef_all.shape[0], arrived.shape[2]), F32)
    for orbit in range(gathered.shape[0]):
        running = running + column[:, orbit : orbit + 1] * jnp.dot(
            coef_all, gathered[orbit], preferred_element_type=F32
        )
    amp_ao = running.astype(BF16)
    per_func = jnp.einsum("xnp,np->xn", deriv, amp_ao, preferred_element_type=F32)
    atoms = ATOM_DEV * lax.axis_size("aux") * lax.axis_size("ao")
    onehot = (owner[:, None] == jnp.arange(atoms, dtype=jnp.int32)[None, :]).astype(F32)
    partial_grad = jnp.dot(per_func, onehot, precision=lax.Precision.HIGHEST)
    totals = lax.psum(partial_grad, ("aux", "ao"))
    own = lax.axis_index(("aux", "ao")) * ATOM_DEV
    return amp_ao, lax.dynamic_slice_in_dim(totals, own, ATOM_DEV, 1)


def local(*args):
    aux, ao = lax.axis_size("aux"), lax.axis_size("ao")
    occ, width = args[0].shape[1], args[5].shape[2]
    if ao == 4 and aux * ao * occ <= 512 and occ % 8 == 0 and width % CHUNK == 0:
        return fused(aux, *args)
    return staged(*args)


def solution(mesh):
    return jax.shard_map(
        local,
        mesh=mesh,
        in_specs=(
            P(("batch", "ao"), "aux", None),
            P(("batch", "ao")),
            P("aux"),
            P("ao", "aux"),
            P("ao", "batch"),
            P(None, "ao", "aux"),
            P("ao"),
        ),
        out_specs=(P(("batch", "ao"), "aux"), P(None, ("batch", "aux", "ao"))),
        check_vma=False,
    )
```

```python
import functools

import jax
import jax.numpy as jnp
from jax import lax
from jax.experimental import pallas as pl
from jax.experimental.pallas import tpu as pltpu
from jax.sharding import PartitionSpec as P

ATOM_DEV = 3
MESH = pl.DeviceIdType.MESH
F32 = jnp.float32
BF16 = jnp.bfloat16
CHUNK = 512
ROWS = 256
SLOTS = 3
LEAVE = 8


def eye(rows, columns, dtype):
    row = lax.broadcasted_iota(jnp.int32, (rows, columns), 0)
    column = lax.broadcasted_iota(jnp.int32, (rows, columns), 1)
    return (row == column).astype(F32).astype(dtype)


def across(left, right, **kw):
    return lax.dot_general(
        left, right, (((1,), (1,)), ((), ())), preferred_element_type=F32, **kw
    )


def fused_kernel(
    aux, atoms, pair, batch_energy, occ_energy, occ_coef, batch_coef, deriv, owner,
    amp, grad,
    shares, outgoing, arrived, coef, coef_t, weights, packed, slabs, total,
    z_send, z_recv, w_send, w_recv, x_send, x_recv, c_send, c_recv, f_send, f_recv, s_send, s_recv, d_sem,
):
    occ = pair.shape[1]
    width = pair.shape[2] // aux
    chunks = width // CHUNK
    half = CHUNK // 2
    functions = occ_coef.shape[1]
    me_z, me = lax.axis_index("aux"), lax.axis_index("ao")
    far = lax.rem(me + 2, 4)
    near = me + 1 - 2 * lax.rem(me, 2)
    near_far = lax.rem(near + 2, 4)

    def fetch(step):
        return pltpu.make_async_copy(
            deriv.at[:, :, pl.ds(step * CHUNK, CHUNK)], slabs.at[step % SLOTS], d_sem.at[step % SLOTS]
        )

    for step in range(min(SLOTS, chunks)):
        fetch(step).start()

    barrier = pltpu.get_barrier_semaphore()
    for hop in range(1, aux):
        pl.semaphore_signal(
            barrier, inc=1, device_id={"aux": lax.rem(me_z + hop, aux)}, device_id_type=MESH
        )
    for other in (far, near, near_far):
        pl.semaphore_signal(barrier, inc=1, device_id={"ao": other}, device_id_type=MESH)

    turned = occ_coef[...].astype(F32)
    coef[me_z] = jnp.concatenate(
        [turned[:, : functions // 2], turned[:, functions // 2 :]], axis=0
    ).astype(BF16)

    scale_row = 2.0 / (batch_energy[0] + occ_energy[...])
    scale = jnp.sum(eye(occ, occ, F32) * scale_row, axis=1, keepdims=True)

    def form(z, step):
        start = pl.multiple_of(z * width + step * CHUNK, CHUNK)
        block = pair[0, :, pl.ds(start, CHUNK)].astype(F32) * scale
        return jnp.concatenate([block[:, :half], block[:, half:]], axis=0).astype(BF16)

    def z_copy(step, hop, source=None):
        z = me_z if source is None else source
        return pltpu.make_async_remote_copy(
            src_ref=outgoing.at[hop - 1, step],
            dst_ref=arrived.at[step, me, z],
            send_sem=z_send.at[step, hop - 1],
            recv_sem=z_recv.at[step, hop - 1],
            device_id={"aux": lax.rem(me_z + hop, aux)},
            device_id_type=MESH,
        )

    def w_copy(hop, source=None):
        z = me_z if source is None else source
        return pltpu.make_async_remote_copy(
            src_ref=coef.at[me_z],
            dst_ref=coef.at[z],
            send_sem=w_send.at[hop - 1],
            recv_sem=w_recv.at[hop - 1],
            device_id={"aux": lax.rem(me_z + hop, aux)},
            device_id_type=MESH,
        )

    def slot_copy(step, slot, sends, recvs, target, source=None):
        return pltpu.make_async_remote_copy(
            src_ref=arrived.at[step, slot],
            dst_ref=arrived.at[step, slot if source is None else source],
            send_sem=sends.at[step],
            recv_sem=recvs.at[step],
            device_id={"ao": target},
            device_id_type=MESH,
        )

    def x_copy(step, source=None):
        return slot_copy(step, me, x_send, x_recv, far, source)

    def c_copy(step, source=None):
        return slot_copy(step, me, c_send, c_recv, near, source)

    def f_copy(step, source=None):
        return slot_copy(step, far, f_send, f_recv, near, source)

    def send_chunk(step):
        for hop in range(1, aux):
            outgoing[hop - 1, step] = form(lax.rem(me_z + hop, aux), step)
            z_copy(step, hop).start()
        arrived[step, me, me_z] = form(me_z, step)

    def behind(hop):
        return lax.rem(me_z + aux - hop, aux)

    pl.semaphore_wait(barrier, aux + 2)
    send_chunk(0)
    for hop in range(1, aux):
        w_copy(hop).start()
    for step in range(1, chunks):
        send_chunk(step)

    total[...] = jnp.zeros_like(total)
    columns = batch_coef[...].astype(F32)

    def build_weights():
        for hop in range(1, aux):
            w_copy(hop, behind(hop)).wait_recv()
        for part in range(2):
            lanes = slice(part * (functions // 2), (part + 1) * (functions // 2))
            for z in range(aux):
                block = coef[z].astype(F32)[part * occ : (part + 1) * occ]
                for orbit in range(4):
                    first = (orbit * aux + z) * occ
                    coef_t[first : first + occ, :] = block * columns[orbit : orbit + 1, lanes]
            weights[lanes, :] = coef_t[...].T.astype(BF16)

    def compute(step):
        for pair_of in range(2 * aux):
            blocks = [
                arrived[step, source // aux, source % aux].astype(F32)
                for source in (2 * pair_of, 2 * pair_of + 1)
            ]
            for part in range(2):
                packed[2 * occ * pair_of : 2 * occ * (pair_of + 1), part * half : (part + 1) * half] = (
                    jnp.concatenate(
                        [block[part * occ : (part + 1) * occ] for block in blocks], axis=0
                    ).astype(BF16)
                )
        fetch(step).wait()
        slab = slabs.at[step % SLOTS]

        @pl.loop(0, functions // ROWS)
        def _(index):
            rows = pl.ds(pl.multiple_of(index * ROWS, ROWS), ROWS)
            rounded = jnp.dot(
                weights[rows, :], packed[...], preferred_element_type=F32
            ).astype(BF16)
            amp[rows, step * CHUNK : (step + 1) * CHUNK] = rounded
            wide = rounded.astype(F32)
            for axis_dir in range(3):
                product = slab[axis_dir, rows, :].astype(F32) * wide
                lanes = product[:, :128]
                for first in range(128, CHUNK, 128):
                    lanes = lanes + product[:, first : first + 128]
                total[axis_dir, rows, :] += lanes

        if step + SLOTS < chunks:
            fetch(step + SLOTS).start()

    for turn in range(chunks + 2):
        if turn < chunks:
            for hop in range(1, aux):
                z_copy(turn, hop, behind(hop)).wait_recv()
            x_copy(turn).start()
            c_copy(turn).start()
        if turn == 0:
            build_weights()
        if 1 <= turn <= chunks:
            x_copy(turn - 1, far).wait_recv()
            f_copy(turn - 1).start()
        if turn >= 2:
            c_copy(turn - 2, near).wait_recv()
            f_copy(turn - 2, near_far).wait_recv()
            compute(turn - 2)

    atom = lax.broadcasted_iota(jnp.int32, (atoms, functions), 0)
    onehot = (owner[...][None, :] == atom).astype(F32)
    sums = jnp.concatenate(
        [
            jnp.dot(onehot, total[axis_dir], precision=lax.Precision.HIGHEST, preferred_element_type=F32)
            for axis_dir in range(3)
        ],
        axis=0,
    )
    shares[0, me_z] = across(jnp.ones((8, 128), F32), sums, precision=lax.Precision.HIGHEST)

    def s_copy(level, hop, mine, count, name, source=None):
        return pltpu.make_async_remote_copy(
            src_ref=shares.at[level, mine],
            dst_ref=shares.at[level, mine if source is None else source],
            send_sem=s_send.at[level, hop - 1],
            recv_sem=s_recv.at[level, hop - 1],
            device_id={name: lax.rem(mine + hop, count)},
            device_id_type=MESH,
        )

    for level, (mine, count, name) in enumerate(((me_z, aux, "aux"), (me, 4, "ao"))):
        if level == 1:
            shares[1, me] = functools.reduce(lambda a, b: a + b, [shares[0, z] for z in range(aux)])
        for hop in range(1, count):
            s_copy(level, hop, mine, count, name).start()
        for hop in range(1, count):
            s_copy(level, hop, mine, count, name, lax.rem(mine + count - hop, count)).wait_recv()
    grad[...] = functools.reduce(lambda a, b: a + b, [shares[1, ao] for ao in range(4)])
    for level, (mine, count, name) in enumerate(((me_z, aux, "aux"), (me, 4, "ao"))):
        for hop in range(1, count):
            s_copy(level, hop, mine, count, name).wait_send()

    for hop in range(1, aux):
        w_copy(hop).wait_send()
    for step in range(chunks):
        for hop in range(1, aux):
            z_copy(step, hop).wait_send()
        x_copy(step).wait_send()
        c_copy(step).wait_send()
        f_copy(step).wait_send()


def leave_kernel(held, sums, out, sums_out, sems):
    rows = held.shape[0] // LEAVE
    copies = [
        pltpu.make_async_copy(
            held.at[pl.ds(part * rows, rows)], out.at[pl.ds(part * rows, rows)], sems.at[part]
        )
        for part in range(LEAVE)
    ]
    for copy in copies:
        copy.start()
    sums_out[...] = sums[...]
    for copy in copies:
        copy.wait()


def fused(aux, pair_ints, batch_energy, occ_energy, occ_coef, batch_coef, deriv, owner):
    occ = pair_ints.shape[1]
    functions, width = deriv.shape[1], deriv.shape[2]
    chunks = width // CHUNK
    atoms = ATOM_DEV * aux * 4
    depth = 4 * aux * occ
    vmem = pl.BlockSpec(memory_space=pltpu.VMEM)
    dma = pltpu.SemaphoreType.DMA
    amp, grad = pl.pallas_call(
        functools.partial(fused_kernel, aux, atoms),
        out_shape=(
            pltpu.VMEM((functions, width), BF16),
            jax.ShapeDtypeStruct((8, 3 * atoms), F32),
        ),
        in_specs=[
            vmem,
            pl.BlockSpec(memory_space=pltpu.SMEM),
            vmem,
            vmem,
            vmem,
            pl.BlockSpec(memory_space=pl.ANY),
            vmem,
        ],
        out_specs=(vmem, vmem),
        scratch_shapes=[
            pltpu.VMEM((2, max(aux, 4), 8, 3 * atoms), F32),
            pltpu.VMEM((aux - 1, chunks, 2 * occ, CHUNK // 2), BF16),
            pltpu.VMEM((chunks, 4, aux, 2 * occ, CHUNK // 2), BF16),
            pltpu.VMEM((aux, 2 * occ, functions // 2), BF16),
            pltpu.VMEM((depth, functions // 2), F32),
            pltpu.VMEM((functions, depth), BF16),
            pltpu.VMEM((depth, CHUNK), BF16),
            pltpu.VMEM((SLOTS, 3, functions, CHUNK), BF16),
            pltpu.VMEM((3, functions, 128), F32),
            dma((chunks, aux - 1)),
            dma((chunks, aux - 1)),
            dma((aux - 1,)),
            dma((aux - 1,)),
            dma((chunks,)),
            dma((chunks,)),
            dma((chunks,)),
            dma((chunks,)),
            dma((chunks,)),
            dma((chunks,)),
            dma((2, max(aux, 4) - 1)),
            dma((2, max(aux, 4) - 1)),
            dma((SLOTS,)),
        ],
        compiler_params=pltpu.CompilerParams(
            collective_id=0, has_side_effects=True, vmem_limit_bytes=42 << 20
        ),
    )(
        pair_ints,
        batch_energy,
        occ_energy.reshape(1, -1),
        occ_coef.T,
        batch_coef.T,
        deriv,
        owner,
    )
    amp, grad = pl.pallas_call(
        leave_kernel,
        out_shape=(
            jax.ShapeDtypeStruct((functions, width), BF16),
            jax.ShapeDtypeStruct(grad.shape, F32),
        ),
        in_specs=[vmem, vmem],
        out_specs=(pl.BlockSpec(memory_space=pl.ANY), vmem),
        scratch_shapes=[dma((LEAVE,))],
        compiler_params=pltpu.CompilerParams(vmem_limit_bytes=1 << 20),
    )(amp, grad)
    totals = grad[0].reshape(3, atoms)
    own = lax.axis_index(("aux", "ao")) * ATOM_DEV
    return amp, lax.dynamic_slice_in_dim(totals, own, ATOM_DEV, 1)


def staged(pair_ints, batch_energy, occ_energy, occ_coef, batch_coef, deriv, owner):
    scale = 2.0 / (batch_energy[:, None] + occ_energy[None, :])
    formed = (pair_ints.astype(F32) * scale[:, :, None]).astype(BF16)
    arrived = lax.all_to_all(formed, "aux", split_axis=2, concat_axis=1, tiled=True)
    coef_all = lax.all_gather(occ_coef, "aux", axis=1, tiled=True)
    column = batch_coef.astype(F32)
    gathered = lax.all_gather(arrived, "ao", axis=0, tiled=True)
    running = jnp.zeros((coef_all.shape[0], arrived.shape[2]), F32)
    for orbit in range(gathered.shape[0]):
        running = running + column[:, orbit : orbit + 1] * jnp.dot(
            coef_all, gathered[orbit], preferred_element_type=F32
        )
    amp_ao = running.astype(BF16)
    per_func = jnp.einsum("xnp,np->xn", deriv, amp_ao, preferred_element_type=F32)
    atoms = ATOM_DEV * lax.axis_size("aux") * lax.axis_size("ao")
    onehot = (owner[:, None] == jnp.arange(atoms, dtype=jnp.int32)[None, :]).astype(F32)
    partial_grad = jnp.dot(per_func, onehot, precision=lax.Precision.HIGHEST)
    totals = lax.psum(partial_grad, ("aux", "ao"))
    own = lax.axis_index(("aux", "ao")) * ATOM_DEV
    return amp_ao, lax.dynamic_slice_in_dim(totals, own, ATOM_DEV, 1)


def local(*args):
    aux, ao = lax.axis_size("aux"), lax.axis_size("ao")
    occ, width = args[0].shape[1], args[5].shape[2]
    if ao == 4 and aux * ao * occ <= 512 and occ % 8 == 0 and width % CHUNK == 0:
        return fused(aux, *args)
    return staged(*args)


def solution(mesh):
    return jax.shard_map(
        local,
        mesh=mesh,
        in_specs=(
            P(("batch", "ao"), "aux", None),
            P(("batch", "ao")),
            P("aux"),
            P("ao", "aux"),
            P("ao", "batch"),
            P(None, "ao", "aux"),
            P("ao"),
        ),
        out_specs=(P(("batch", "ao"), "aux"), P(None, ("batch", "aux", "ao"))),
        check_vma=False,
    )
```
